32 devices in a mesh: src: 8 (over y, x, core), rcv: 4 (over z).
Axes of the slice: x: 2, y: 2, z: 4, core: 2. Of those that a mesh axis runs over, the one named last changes fastest.
Arguments:
- data: bfloat16 [2, 6144, 6144], P(None, 'src', 'rcv'), may hold values from -24 to 24
- source_term: float32 [2, 6144], P(None, 'src'), may hold values from -1 to 1
Outputs:
- matched: bfloat16 [2, 6144, 6144], P(None, 'src', 'rcv')
The draws below stay inside these ranges and needn't reach their ends.
All inputs are finite; a program needn't handle non-finite values.
Results may differ from the reference program's by a relative error of at most 0.0057.
Values may be sent and summed in bfloat16 or wider, within the bound.
A program may use at most 128 MiB of HBM per device.

```python
import math
import jax
import jax.numpy as jnp

NS = 6144
LINE = 64


def source_values(key):
    base = jax.random.fold_in(key, 101)
    key_amp, key_phase = jax.random.split(base)
    amplitude = jnp.exp(jax.random.uniform(key_amp, (NS,), jnp.float32, math.log(0.5), math.log(2.0))) / math.sqrt(NS)
    phase = jax.random.uniform(key_phase, (NS,), jnp.float32, -math.pi, math.pi)
    return jnp.stack([amplitude * jnp.cos(phase), amplitude * jnp.sin(phase)])


def draw_source_term(key, part):
    return source_values(key)


def draw_data(key, part):
    weights = source_values(key)
    base = jax.random.fold_in(key, 202)
    key_wave, key_gain = jax.random.split(base)
    direct = 0.5 * jax.random.normal(key_wave, (2, NS, NS), jnp.float32)
    gain_low = 0.25
    right_re = weights[0][:, None] * direct[0] - weights[1][:, None] * direct[1]
    right_im = weights[0][:, None] * direct[1] + weights[1][:, None] * direct[0]
    echo_re = jnp.dot(direct[0], right_re) - jnp.dot(direct[1], right_im)
    echo_im = jnp.dot(direct[0], right_im) + jnp.dot(direct[1], right_re)
    lines = NS // LINE
    gain = jnp.exp(jax.random.uniform(key_gain, (lines, lines), jnp.float32, math.log(gain_low), math.log(2.5)))
    spread = jnp.repeat(jnp.repeat(gain, LINE, axis=0), LINE, axis=1)
    return (spread[None] * (direct + jnp.stack([echo_re, echo_im]))).astype(jnp.bfloat16)


def setup_inputs(seed: int = 0) -> dict:
    splits = jax.random.split(jax.random.key(seed), 3)
    data = draw_data(jax.random.fold_in(splits[2], 71), 0)
    source_term = draw_source_term(jax.random.fold_in(splits[2], 71), 0)
    return {"data": data, "source_term": source_term}


def line_block_sums(multiples, data):
    mult = multiples.astype(jnp.float32)
    recorded = data.astype(jnp.float32)
    cross_re = mult[0] * recorded[0] + mult[1] * recorded[1]
    cross_im = mult[0] * recorded[1] - mult[1] * recorded[0]
    energy = mult[0] * mult[0] + mult[1] * mult[1]
    stacked = jnp.stack([cross_re, cross_im, energy])
    height = stacked.shape[1] // LINE
    breadth = stacked.shape[2] // LINE
    return stacked.reshape(3, height, LINE, breadth, LINE).sum(axis=(2, 4))


def reference(data, source_term):
    recorded = data.astype(jnp.float32)
    weight_re = source_term[0][:, None]
    weight_im = source_term[1][:, None]
    scaled_re = (weight_re * recorded[0] - weight_im * recorded[1]).astype(jnp.bfloat16)
    scaled_im = (weight_re * recorded[1] + weight_im * recorded[0]).astype(jnp.bfloat16)
    product_re = jnp.dot(data[0], scaled_re, preferred_element_type=jnp.float32) - jnp.dot(data[1], scaled_im, preferred_element_type=jnp.float32)
    product_im = jnp.dot(data[0], scaled_im, preferred_element_type=jnp.float32) + jnp.dot(data[1], scaled_re, preferred_element_type=jnp.float32)
    multiples = jnp.stack([product_re, product_im]).astype(jnp.bfloat16)
    sums = line_block_sums(multiples, data)
    count = sums.shape[1]
    padded = jnp.pad(sums, ((0, 0), (1, 1), (1, 1)))
    window = jnp.zeros_like(sums)
    for shift_row in range(3):
        for shift_col in range(3):
            window = window + padded[:, shift_row:shift_row + count, shift_col:shift_col + count]
    filter_re = window[0] / (window[2] + 1e-5)
    filter_im = window[1] / (window[2] + 1e-5)
    mult = multiples.astype(jnp.float32).reshape(2, count, LINE, count, LINE)
    coef_re = filter_re[:, None, :, None]
    coef_im = filter_im[:, None, :, None]
    matched_re = coef_re * mult[0] - coef_im * mult[1]
    matched_im = coef_re * mult[1] + coef_im * mult[0]
    matched = jnp.stack([matched_re, matched_im]).reshape(2, NS, NS)
    return matched.astype(jnp.bfloat16)
```

```python
import functools

import jax
import jax.numpy as jnp
from jax import lax
from jax.experimental import pallas as pl
from jax.experimental.pallas import tpu as pltpu
from jax.sharding import PartitionSpec as P

LINE = 64


stabiliser = 1e-05


def with_halo(block, sides, width):
    for axis, dim in sides:
        count = lax.axis_size(axis)
        forward = [(i, i + 1) for i in range(count - 1)]
        backward = [(target, source) for source, target in forward]
        low = lax.ppermute(
            lax.slice_in_dim(block, block.shape[dim] - width, None, axis=dim), axis, forward
        )
        high = lax.ppermute(lax.slice_in_dim(block, 0, width, axis=dim), axis, backward)
        block = jnp.concatenate([low, block, high], axis=dim)
    return block


def largest(size, choices):
    return next(c for c in choices if size % c == 0)


def product_kernel(options, tile_rows, last, block_of, choice_of, *refs):
    count = 1 + max(max(o) for o in options)
    blocks, rest = refs[:count], list(refs[count:])
    right_ref = rest.pop(0)
    if last:
        total_ref, data_ref, out_ref, sums_ref, left, sems = rest
    else:
        out_ref, left, sems = rest
    phase = pl.program_id(1)
    parts, depth = right_ref.shape[0], right_ref.shape[2]

    @pl.when(jnp.logical_and(pl.program_id(0) == 0, phase == 0))
    def _():
        for p, allowed in enumerate(options):
            for c in allowed:
                @pl.when(choice_of[p] == c)
                def _():
                    pltpu.make_async_copy(blocks[c], left.at[p], sems.at[p]).start()

    @pl.when(pl.program_id(0) == 0)
    def _():
        pltpu.make_async_copy(blocks[0], left.at[phase], sems.at[phase]).wait()

    def products(rows):
        real_part = imag_part = None
        for q in range(parts):
            span = slice(q * depth, (q + 1) * depth)
            a_re, a_im = left[phase, 0, rows, span], left[phase, 1, rows, span]
            b_re, b_im = right_ref[q, 0], right_ref[q, 1]
            dot = functools.partial(jnp.dot, preferred_element_type=jnp.float32)
            re = dot(a_re, b_re) - dot(a_im, b_im)
            im = dot(a_re, b_im) + dot(a_im, b_re)
            real_part = re if q == 0 else real_part + re
            imag_part = im if q == 0 else imag_part + im
        return real_part, imag_part

    tiles = left.shape[2] // tile_rows

    @pl.loop(0, tiles)
    def _(tile):
        rows = pl.ds(pl.multiple_of(tile * tile_rows, tile_rows), tile_rows)
        re, im = products(rows)
        if last:
            re = (re + total_ref[0, rows, :]).astype(jnp.bfloat16)
            im = (im + total_ref[1, rows, :]).astype(jnp.bfloat16)
            out_ref[0, rows, :] = re
            out_ref[1, rows, :] = im
            re, im = re.astype(jnp.float32), im.astype(jnp.float32)
            d_re = data_ref[0, rows, :].astype(jnp.float32)
            d_im = data_ref[1, rows, :].astype(jnp.float32)
            terms = (re * d_re + im * d_im, re * d_im - im * d_re, re * re + im * im)
            for t, term in enumerate(terms):
                folded = term.reshape(tile_rows // LINE, LINE, term.shape[1])
                sums_ref[tile, t] = folded.sum(axis=1)
        else:
            @pl.when(phase == 0)
            def _():
                out_ref[0, rows, :] = re
                out_ref[1, rows, :] = im

            @pl.when(phase > 0)
            def _():
                out_ref[0, rows, :] += re
                out_ref[1, rows, :] += im


def multiply(blocks, options, block_of, choice_of, panel, total=None, data=None):
    last = total is not None
    _, rows, width = blocks[0].shape
    depth, columns = panel.shape[2], panel.shape[3]
    parts = width // depth
    wide = largest(columns, (512, 384, 256, 128))
    tile_rows = largest(rows, (256, 128, 64))
    tiles = rows // tile_rows
    phases = len(options)

    def column(j, p, *_):
        return (0, 0, j)

    whole = pl.BlockSpec((2, rows, wide), column)
    in_specs = [pl.BlockSpec(memory_space=pl.ANY)] * len(blocks) + [
        pl.BlockSpec((parts, 2, depth, wide), lambda j, p, b, c: (b[p], 0, 0, j))
    ]
    operands = list(blocks) + [panel]
    if last:
        in_specs += [whole, whole]
        operands += [total, data]
        lines = tile_rows // LINE
        out_shape = (
            jax.ShapeDtypeStruct((2, rows, columns), jnp.bfloat16),
            jax.ShapeDtypeStruct((tiles, 3, lines, columns), jnp.float32),
        )
        out_specs = (
            whole,
            pl.BlockSpec((tiles, 3, lines, wide), lambda j, p, *_: (0, 0, 0, j)),
        )
    else:
        out_shape = jax.ShapeDtypeStruct((2, rows, columns), jnp.float32)
        out_specs = whole
    return pl.pallas_call(
        functools.partial(product_kernel, options, tile_rows, last),
        out_shape=out_shape,
        grid_spec=pltpu.PrefetchScalarGridSpec(
            num_scalar_prefetch=2,
            grid=(columns // wide, phases),
            in_specs=in_specs,
            out_specs=out_specs,
            scratch_shapes=[
                pltpu.VMEM((phases, 2, rows, width), jnp.bfloat16),
                pltpu.SemaphoreType.DMA((phases,)),
            ],
        ),
        compiler_params=pltpu.CompilerParams(vmem_limit_bytes=48 << 20),
        cost_estimate=pl.CostEstimate(
            flops=8 * rows * width * columns * phases,
            bytes_accessed=4 * phases * rows * width + 4 * phases * width * columns,
            transcendentals=0,
        ),
    )(block_of, choice_of, *operands)


def on_device(data, source_term):
    _, row_count, col_count = data.shape
    count = lax.axis_size("rcv")
    place = lax.axis_index("rcv")
    recorded = data.astype(jnp.float32)
    weight_re = source_term[0][:, None]
    weight_im = source_term[1][:, None]
    scaled = jnp.stack(
        [
            weight_re * recorded[0] - weight_im * recorded[1],
            weight_re * recorded[1] + weight_im * recorded[0],
        ]
    ).astype(jnp.bfloat16)
    panel = lax.all_gather(scaled, "src", axis=0)

    upward = [(i, i + 1) for i in range(count - 1)]
    downward = [(i + 1, i) for i in range(count - 1)]
    ups, downs = [data], [data]
    for _ in range(count - 1):
        ups.append(lax.ppermute(ups[-1], "rcv", upward))
        downs.append(lax.ppermute(downs[-1], "rcv", downward))

    def block_at(step):
        return jnp.where(step <= place, place - step, step)

    inner = count - 2
    blocks = [data] + ups[1 : inner + 1] + downs[1 : inner + 1]
    options = [(0,)] + [
        (step,) + tuple(inner + m for m in range(1, step + 1)) for step in range(1, inner + 1)
    ]
    block_of = jnp.stack([block_at(step) for step in range(inner + 1)]).astype(jnp.int32)
    choice_of = jnp.stack(
        [jnp.where(step <= place, step, inner + step - place) for step in range(inner + 1)]
    ).astype(jnp.int32)
    total = multiply(blocks, options, block_of, choice_of, panel)
    end = count - 1
    multiples, row_sums = multiply(
        [ups[end]] + downs[1:],
        [tuple(range(count))],
        block_at(end).reshape(1).astype(jnp.int32),
        jnp.where(end <= place, 0, end - place).reshape(1).astype(jnp.int32),
        panel,
        total,
        data,
    )

    block_rows = row_count // LINE
    block_cols = col_count // LINE
    local_sums = row_sums.transpose(1, 0, 2, 3).reshape(3, block_rows, block_cols, LINE).sum(axis=3)
    sums = with_halo(local_sums, (("src", 1), ("rcv", 2)), 1)
    window = jnp.zeros((3, block_rows, block_cols), jnp.float32)
    for shift_row in range(3):
        for shift_col in range(3):
            window = (
                window
                + sums[:, shift_row : shift_row + block_rows, shift_col : shift_col + block_cols]
            )
    coef = jnp.repeat(window[:2] / (window[2:] + stabiliser), LINE, axis=2)
    mult = multiples.reshape(2, block_rows, LINE, col_count).astype(jnp.float32)
    coef_re = coef[0][:, None, :]
    coef_im = coef[1][:, None, :]
    matched = jnp.stack(
        [coef_re * mult[0] - coef_im * mult[1], coef_re * mult[1] + coef_im * mult[0]]
    )
    return matched.astype(jnp.bfloat16).reshape(2, row_count, col_count)


def solution(mesh):
    in_specs = (P(None, "src", "rcv"), P(None, "src"))
    out_specs = P(None, "src", "rcv")
    return jax.shard_map(
        on_device, mesh=mesh, in_specs=in_specs, out_specs=out_specs, check_vma=False
    )
```

```python
import functools

import jax
import jax.numpy as jnp
from jax import lax
from jax.experimental import pallas as pl
from jax.experimental.pallas import tpu as pltpu
from jax.sharding import PartitionSpec as P

LINE = 64


stabiliser = 1e-05


def with_halo(block, sides, width):
    for axis, dim in sides:
        count = lax.axis_size(axis)
        forward = [(i, i + 1) for i in range(count - 1)]
        backward = [(target, source) for source, target in forward]
        low = lax.ppermute(
            lax.slice_in_dim(block, block.shape[dim] - width, None, axis=dim), axis, forward
        )
        high = lax.ppermute(lax.slice_in_dim(block, 0, width, axis=dim), axis, backward)
        block = jnp.concatenate([low, block, high], axis=dim)
    return block


def largest(size, choices):
    return next(c for c in choices if size % c == 0)


def product_kernel(options, tile_rows, last, handed, pieces, block_of, choice_of, *refs):
    count = pieces * (1 + max(max(o) for o in options))
    blocks, rest = refs[:count], list(refs[count:])
    right_ref = rest.pop(0)
    if last:
        total_ref, data_ref = rest.pop(0), rest.pop(0)
        if handed:
            rest.pop(0)
        out_ref, sums_ref, left, sems = rest
    else:
        out_ref, left, sems = rest
    phase = pl.program_id(1)
    parts, depth = right_ref.shape[0], right_ref.shape[2]

    def load(c, p, piece):
        start = sum(blocks[i].shape[1] for i in range(piece))
        source = blocks[c * pieces + piece]
        rows = pl.ds(start, source.shape[1])
        return pltpu.make_async_copy(source, left.at[p, :, rows], sems.at[p, piece])

    @pl.when(jnp.logical_and(pl.program_id(0) == 0, phase == 0))
    def _():
        for p, allowed in enumerate(options):
            for c in allowed:
                @pl.when(choice_of[p] == c)
                def _():
                    for piece in range(pieces):
                        load(c, p, piece).start()

    @pl.when(pl.program_id(0) == 0)
    def _():
        for piece in range(pieces):
            load(0, phase, piece).wait()

    def products(rows):
        real_part = imag_part = None
        for q in range(parts):
            span = slice(q * depth, (q + 1) * depth)
            a_re, a_im = left[phase, 0, rows, span], left[phase, 1, rows, span]
            b_re, b_im = right_ref[q, 0], right_ref[q, 1]
            dot = functools.partial(jnp.dot, preferred_element_type=jnp.float32)
            re = dot(a_re, b_re) - dot(a_im, b_im)
            im = dot(a_re, b_im) + dot(a_im, b_re)
            real_part = re if q == 0 else real_part + re
            imag_part = im if q == 0 else imag_part + im
        return real_part, imag_part

    tiles = left.shape[2] // tile_rows

    @pl.loop(0, tiles)
    def _(tile):
        rows = pl.ds(pl.multiple_of(tile * tile_rows, tile_rows), tile_rows)
        re, im = products(rows)
        if last:
            re = (re + total_ref[0, rows, :]).astype(jnp.bfloat16)
            im = (im + total_ref[1, rows, :]).astype(jnp.bfloat16)
            out_ref[0, rows, :] = re
            out_ref[1, rows, :] = im
            re, im = re.astype(jnp.float32), im.astype(jnp.float32)
            d_re = data_ref[0, rows, :].astype(jnp.float32)
            d_im = data_ref[1, rows, :].astype(jnp.float32)
            terms = (re * d_re + im * d_im, re * d_im - im * d_re, re * re + im * im)
            for t, term in enumerate(terms):
                folded = term.reshape(tile_rows // LINE, LINE, term.shape[1])
                sums_ref[tile, t] = folded.sum(axis=1)
        else:
            @pl.when(phase == 0)
            def _():
                out_ref[0, rows, :] = re
                out_ref[1, rows, :] = im

            @pl.when(phase > 0)
            def _():
                out_ref[0, rows, :] += re
                out_ref[1, rows, :] += im


def multiply(blocks, options, block_of, choice_of, panel, first_row=0, last=None):
    pieces = len(blocks[0])
    rows = sum(piece.shape[1] for piece in blocks[0])
    width = blocks[0][0].shape[2]
    depth, columns = panel.shape[2], panel.shape[3]
    parts = width // depth
    wide = largest(columns, (512, 384, 256, 128))
    tile_rows = largest(rows, (256, 128, 64))
    tiles = rows // tile_rows
    phases = len(options)
    place = first_row // rows

    whole = pl.BlockSpec((2, rows, wide), lambda j, p, *_: (0, place, j))
    operands = [piece for block in blocks for piece in block] + [panel]
    in_specs = [pl.BlockSpec(memory_space=pl.ANY)] * (len(operands) - 1) + [
        pl.BlockSpec((parts, 2, depth, wide), lambda j, p, b, c: (b[p], 0, 0, j))
    ]
    aliases = {}
    handed = False
    if last is not None:
        total, data, out = last
        operands += [total, data]
        in_specs += [whole, whole]
        if out is not None:
            handed = True
            aliases = {2 + len(operands): 0}
            operands.append(out)
            in_specs.append(pl.BlockSpec(memory_space=pl.ANY))
        lines = tile_rows // LINE
        out_shape = (
            jax.ShapeDtypeStruct(data.shape, jnp.bfloat16),
            jax.ShapeDtypeStruct((tiles, 3, lines, columns), jnp.float32),
        )
        out_specs = (
            whole,
            pl.BlockSpec((tiles, 3, lines, wide), lambda j, p, *_: (0, 0, 0, j)),
        )
    else:
        out_shape = jax.ShapeDtypeStruct((2, rows, columns), jnp.float32)
        out_specs = whole
    return pl.pallas_call(
        functools.partial(product_kernel, options, tile_rows, last is not None, handed, pieces),
        out_shape=out_shape,
        grid_spec=pltpu.PrefetchScalarGridSpec(
            num_scalar_prefetch=2,
            grid=(columns // wide, phases),
            in_specs=in_specs,
            out_specs=out_specs,
            scratch_shapes=[
                pltpu.VMEM((phases, 2, rows, width), jnp.bfloat16),
                pltpu.SemaphoreType.DMA((phases, pieces)),
            ],
        ),
        input_output_aliases=aliases,
        compiler_params=pltpu.CompilerParams(vmem_limit_bytes=48 << 20),
        cost_estimate=pl.CostEstimate(
            flops=8 * rows * width * columns * phases,
            bytes_accessed=4 * phases * rows * width + 4 * phases * width * columns,
            transcendentals=0,
        ),
    )(block_of, choice_of, *operands)


def scale_kernel(data_ref, weight_ref, out_ref):
    d_re = data_ref[0].astype(jnp.float32)
    d_im = data_ref[1].astype(jnp.float32)
    w_re, w_im = weight_ref[0], weight_ref[1]
    out_ref[0] = (w_re * d_re - w_im * d_im).astype(jnp.bfloat16)
    out_ref[1] = (w_re * d_im + w_im * d_re).astype(jnp.bfloat16)


def scale(data, source_term):
    _, rows, columns = data.shape
    tile = largest(rows, (256, 128, 64))
    block = pl.BlockSpec((2, tile, columns), lambda i: (0, i, 0))
    return pl.pallas_call(
        scale_kernel,
        out_shape=jax.ShapeDtypeStruct(data.shape, jnp.bfloat16),
        grid=(rows // tile,),
        in_specs=[block, pl.BlockSpec((2, tile, 1), lambda i: (0, i, 0))],
        out_specs=block,
        compiler_params=pltpu.CompilerParams(vmem_limit_bytes=24 << 20),
        cost_estimate=pl.CostEstimate(
            flops=6 * rows * columns, bytes_accessed=8 * rows * columns, transcendentals=0
        ),
    )(data, source_term[:, :, None])


def match_kernel(mult_ref, coef_ref, out_ref):
    _, lines, columns = coef_ref.shape[1:]
    m_re = mult_ref[0].astype(jnp.float32).reshape(lines, LINE, columns)
    m_im = mult_ref[1].astype(jnp.float32).reshape(lines, LINE, columns)
    c_re, c_im = coef_ref[0, 0][:, None, :], coef_ref[0, 1][:, None, :]
    shape = (lines * LINE, columns)
    out_ref[0] = (c_re * m_re - c_im * m_im).reshape(shape).astype(jnp.bfloat16)
    out_ref[1] = (c_re * m_im + c_im * m_re).reshape(shape).astype(jnp.bfloat16)


def match(multiples, coef):
    _, rows, columns = multiples.shape
    tile = largest(rows, (128, 64))
    lines = tile // LINE
    block = pl.BlockSpec((2, tile, columns), lambda i: (0, i, 0))
    coef = coef.reshape(2, rows // tile, lines, columns).transpose(1, 0, 2, 3)
    return pl.pallas_call(
        match_kernel,
        out_shape=jax.ShapeDtypeStruct(multiples.shape, jnp.bfloat16),
        grid=(rows // tile,),
        in_specs=[block, pl.BlockSpec((1, 2, lines, columns), lambda i: (i, 0, 0, 0))],
        out_specs=block,
        compiler_params=pltpu.CompilerParams(vmem_limit_bytes=24 << 20),
        cost_estimate=pl.CostEstimate(
            flops=6 * rows * columns, bytes_accessed=8 * rows * columns, transcendentals=0
        ),
    )(multiples, coef)


def on_device(data, source_term):
    _, row_count, col_count = data.shape
    count = lax.axis_size("rcv")
    place = lax.axis_index("rcv")
    panel = lax.all_gather(scale(data, source_term), "src", axis=0)

    block_rows = row_count // LINE
    block_cols = col_count // LINE
    third = row_count // 3
    edges = [0, 2 * third, row_count] if block_rows % 3 == 0 else [0, row_count]
    spans = list(zip(edges[:-1], edges[1:]))
    upward = [(i, i + 1) for i in range(count - 1)]
    downward = [(i + 1, i) for i in range(count - 1)]
    own = [lax.slice_in_dim(data, low, high, axis=1) for low, high in spans]
    ups, downs = [own], [own]
    for _ in range(count - 1):
        ups.append([lax.ppermute(piece, "rcv", upward) for piece in ups[-1]])
        downs.append([lax.ppermute(piece, "rcv", downward) for piece in downs[-1]])

    def block_at(step):
        return jnp.where(step <= place, place - step, step)

    inner = count - 2
    blocks = [own] + ups[1 : inner + 1] + downs[1 : inner + 1]
    options = [(0,)] + [
        (step,) + tuple(inner + m for m in range(1, step + 1)) for step in range(1, inner + 1)
    ]
    block_of = jnp.stack([block_at(step) for step in range(inner + 1)]).astype(jnp.int32)
    choice_of = jnp.stack(
        [jnp.where(step <= place, step, inner + step - place) for step in range(inner + 1)]
    ).astype(jnp.int32)
    total = multiply(blocks, options, block_of, choice_of, panel)
    end = count - 1
    multiples, sums_of = None, []
    for index in reversed(range(len(spans))):
        multiples, row_sums = multiply(
            [[block[index]] for block in [ups[end]] + downs[1:]],
            [tuple(range(count))],
            block_at(end).reshape(1).astype(jnp.int32),
            jnp.where(end <= place, 0, end - place).reshape(1).astype(jnp.int32),
            panel,
            spans[index][0],
            (total, data, multiples),
        )
        lines = (spans[index][1] - spans[index][0]) // LINE
        sums_of.insert(0, row_sums.transpose(1, 0, 2, 3).reshape(3, lines, block_cols, LINE).sum(axis=3))

    sums = with_halo(jnp.concatenate(sums_of, axis=1), (("src", 1), ("rcv", 2)), 1)
    window = jnp.zeros((3, block_rows, block_cols), jnp.float32)
    for shift_row in range(3):
        for shift_col in range(3):
            window = (
                window
                + sums[:, shift_row : shift_row + block_rows, shift_col : shift_col + block_cols]
            )
    return match(multiples, jnp.repeat(window[:2] / (window[2:] + stabiliser), LINE, axis=2))


def solution(mesh):
    in_specs = (P(None, "src", "rcv"), P(None, "src"))
    out_specs = P(None, "src", "rcv")
    return jax.shard_map(
        on_device, mesh=mesh, in_specs=in_specs, out_specs=out_specs, check_vma=False
    )
```

```python
import functools

import jax
import jax.numpy as jnp
from jax import lax
from jax.experimental import pallas as pl
from jax.experimental.pallas import tpu as pltpu
from jax.sharding import PartitionSpec as P

LINE = 64


stabiliser = 1e-05


def with_halo(block, sides, width):
    for axis, dim in sides:
        count = lax.axis_size(axis)
        forward = [(i, i + 1) for i in range(count - 1)]
        backward = [(target, source) for source, target in forward]
        low = lax.ppermute(
            lax.slice_in_dim(block, block.shape[dim] - width, None, axis=dim), axis, forward
        )
        high = lax.ppermute(lax.slice_in_dim(block, 0, width, axis=dim), axis, backward)
        block = jnp.concatenate([low, block, high], axis=dim)
    return block


def largest(size, choices):
    return next(c for c in choices if size % c == 0)


def product_kernel(options, tile_rows, last, handed, pieces, block_of, choice_of, *refs):
    count = pieces * (1 + max(max(o) for o in options))
    blocks, rest = refs[:count], list(refs[count:])
    right_ref = rest.pop(0)
    if last:
        total_ref, data_ref = rest.pop(0), rest.pop(0)
        if handed:
            rest.pop(0)
        out_ref, sums_ref, left, sems = rest
    else:
        out_ref, left, sems = rest
    phase = pl.program_id(1)
    parts, depth = right_ref.shape[0], right_ref.shape[2]

    def load(c, p, piece):
        start = sum(blocks[i].shape[1] for i in range(piece))
        source = blocks[c * pieces + piece]
        rows = pl.ds(start, source.shape[1])
        return pltpu.make_async_copy(source, left.at[p, :, rows], sems.at[p, piece])

    @pl.when(jnp.logical_and(pl.program_id(0) == 0, phase == 0))
    def _():
        for p, allowed in enumerate(options):
            for c in allowed:
                @pl.when(choice_of[p] == c)
                def _():
                    for piece in range(pieces):
                        load(c, p, piece).start()

    @pl.when(pl.program_id(0) == 0)
    def _():
        for piece in range(pieces):
            load(0, phase, piece).wait()

    def products(rows):
        real_part = imag_part = None
        for q in range(parts):
            span = slice(q * depth, (q + 1) * depth)
            a_re, a_im = left[phase, 0, rows, span], left[phase, 1, rows, span]
            b_re, b_im = right_ref[q, 0], right_ref[q, 1]
            dot = functools.partial(jnp.dot, preferred_element_type=jnp.float32)
            re = dot(a_re, b_re) - dot(a_im, b_im)
            im = dot(a_re, b_im) + dot(a_im, b_re)
            real_part = re if q == 0 else real_part + re
            imag_part = im if q == 0 else imag_part + im
        return real_part, imag_part

    tiles = left.shape[2] // tile_rows

    @pl.loop(0, tiles)
    def _(tile):
        rows = pl.ds(pl.multiple_of(tile * tile_rows, tile_rows), tile_rows)
        re, im = products(rows)
        if last:
            re = (re + total_ref[0, rows, :]).astype(jnp.bfloat16)
            im = (im + total_ref[1, rows, :]).astype(jnp.bfloat16)
            out_ref[0, rows, :] = re
            out_ref[1, rows, :] = im
            re, im = re.astype(jnp.float32), im.astype(jnp.float32)
            d_re = data_ref[0, rows, :].astype(jnp.float32)
            d_im = data_ref[1, rows, :].astype(jnp.float32)
            terms = (re * d_re + im * d_im, re * d_im - im * d_re, re * re + im * im)
            for t, term in enumerate(terms):
                folded = term.reshape(tile_rows // LINE, LINE, term.shape[1])
                sums_ref[tile, t] = folded.sum(axis=1)
        else:
            @pl.when(phase == 0)
            def _():
                out_ref[0, rows, :] = re
                out_ref[1, rows, :] = im

            @pl.when(phase > 0)
            def _():
                out_ref[0, rows, :] += re
                out_ref[1, rows, :] += im


def multiply(blocks, options, block_of, choice_of, panel, first_row=0, last=None):
    pieces = len(blocks[0])
    rows = sum(piece.shape[1] for piece in blocks[0])
    width = blocks[0][0].shape[2]
    depth, columns = panel.shape[2], panel.shape[3]
    parts = width // depth
    wide = largest(columns, (512, 384, 256, 128))
    tile_rows = largest(rows, (256, 384, 192, 128, 64))
    tiles = rows // tile_rows
    phases = len(options)
    place = first_row // rows

    whole = pl.BlockSpec((2, rows, wide), lambda j, p, *_: (0, place, j))
    operands = [piece for block in blocks for piece in block] + [panel]
    in_specs = [pl.BlockSpec(memory_space=pl.ANY)] * (len(operands) - 1) + [
        pl.BlockSpec((parts, 2, depth, wide), lambda j, p, b, c: (b[p], 0, 0, j))
    ]
    aliases = {}
    handed = False
    if last is not None:
        total, data, out = last
        operands += [total, data]
        in_specs += [whole, whole]
        if out is not None:
            handed = True
            aliases = {2 + len(operands): 0}
            operands.append(out)
            in_specs.append(pl.BlockSpec(memory_space=pl.ANY))
        lines = tile_rows // LINE
        out_shape = (
            jax.ShapeDtypeStruct(data.shape, jnp.bfloat16),
            jax.ShapeDtypeStruct((tiles, 3, lines, columns), jnp.float32),
        )
        out_specs = (
            whole,
            pl.BlockSpec((tiles, 3, lines, wide), lambda j, p, *_: (0, 0, 0, j)),
        )
    else:
        out_shape = jax.ShapeDtypeStruct((2, rows, columns), jnp.float32)
        out_specs = whole
    return pl.pallas_call(
        functools.partial(product_kernel, options, tile_rows, last is not None, handed, pieces),
        out_shape=out_shape,
        grid_spec=pltpu.PrefetchScalarGridSpec(
            num_scalar_prefetch=2,
            grid=(columns // wide, phases),
            in_specs=in_specs,
            out_specs=out_specs,
            scratch_shapes=[
                pltpu.VMEM((phases, 2, rows, width), jnp.bfloat16),
                pltpu.SemaphoreType.DMA((phases, pieces)),
            ],
        ),
        input_output_aliases=aliases,
        compiler_params=pltpu.CompilerParams(vmem_limit_bytes=48 << 20),
        cost_estimate=pl.CostEstimate(
            flops=8 * rows * width * columns * phases,
            bytes_accessed=4 * phases * rows * width + 4 * phases * width * columns,
            transcendentals=0,
        ),
    )(block_of, choice_of, *operands)


def scale_kernel(data_ref, weight_ref, out_ref):
    d_re = data_ref[0].astype(jnp.float32)
    d_im = data_ref[1].astype(jnp.float32)
    w_re, w_im = weight_ref[0], weight_ref[1]
    out_ref[0] = (w_re * d_re - w_im * d_im).astype(jnp.bfloat16)
    out_ref[1] = (w_re * d_im + w_im * d_re).astype(jnp.bfloat16)


def scale(data, source_term):
    _, rows, columns = data.shape
    tile = largest(rows, (256, 128, 64))
    block = pl.BlockSpec((2, tile, columns), lambda i: (0, i, 0))
    return pl.pallas_call(
        scale_kernel,
        out_shape=jax.ShapeDtypeStruct(data.shape, jnp.bfloat16),
        grid=(rows // tile,),
        in_specs=[block, pl.BlockSpec((2, tile, 1), lambda i: (0, i, 0))],
        out_specs=block,
        compiler_params=pltpu.CompilerParams(vmem_limit_bytes=24 << 20),
        cost_estimate=pl.CostEstimate(
            flops=6 * rows * columns, bytes_accessed=8 * rows * columns, transcendentals=0
        ),
    )(data, source_term[:, :, None])


def match_kernel(mult_ref, coef_ref, out_ref):
    _, lines, columns = coef_ref.shape[1:]
    m_re = mult_ref[0].astype(jnp.float32).reshape(lines, LINE, columns)
    m_im = mult_ref[1].astype(jnp.float32).reshape(lines, LINE, columns)
    c_re, c_im = coef_ref[0, 0][:, None, :], coef_ref[0, 1][:, None, :]
    shape = (lines * LINE, columns)
    out_ref[0] = (c_re * m_re - c_im * m_im).reshape(shape).astype(jnp.bfloat16)
    out_ref[1] = (c_re * m_im + c_im * m_re).reshape(shape).astype(jnp.bfloat16)


def match(multiples, coef):
    _, rows, columns = multiples.shape
    tile = largest(rows, (128, 64))
    lines = tile // LINE
    block = pl.BlockSpec((2, tile, columns), lambda i: (0, i, 0))
    coef = coef.reshape(2, rows // tile, lines, columns).transpose(1, 0, 2, 3)
    return pl.pallas_call(
        match_kernel,
        out_shape=jax.ShapeDtypeStruct(multiples.shape, jnp.bfloat16),
        grid=(rows // tile,),
        in_specs=[block, pl.BlockSpec((1, 2, lines, columns), lambda i: (i, 0, 0, 0))],
        out_specs=block,
        compiler_params=pltpu.CompilerParams(vmem_limit_bytes=24 << 20),
        cost_estimate=pl.CostEstimate(
            flops=6 * rows * columns, bytes_accessed=8 * rows * columns, transcendentals=0
        ),
    )(multiples, coef)


def on_device(data, source_term):
    _, row_count, col_count = data.shape
    count = lax.axis_size("rcv")
    place = lax.axis_index("rcv")
    block_rows = row_count // LINE
    block_cols = col_count // LINE
    half = row_count // 2
    edges = [0, half, row_count] if block_rows % 2 == 0 else [0, row_count]
    spans = list(zip(edges[:-1], edges[1:]))
    upward = [(i, i + 1) for i in range(count - 1)]
    downward = [(i + 1, i) for i in range(count - 1)]
    own = [lax.slice_in_dim(data, low, high, axis=1) for low, high in spans]
    panel = lax.all_gather(scale(data, source_term), "src", axis=0)
    ups, downs = [own], [own]
    for _ in range(count - 1):
        ups.append([lax.ppermute(piece, "rcv", upward) for piece in ups[-1]])
        downs.append([lax.ppermute(piece, "rcv", downward) for piece in downs[-1]])

    def block_at(step):
        return jnp.where(step <= place, place - step, step)

    inner = count - 2
    blocks = [own] + ups[1 : inner + 1] + downs[1 : inner + 1]
    options = [(0,)] + [
        (step,) + tuple(inner + m for m in range(1, step + 1)) for step in range(1, inner + 1)
    ]
    block_of = jnp.stack([block_at(step) for step in range(inner + 1)]).astype(jnp.int32)
    choice_of = jnp.stack(
        [jnp.where(step <= place, step, inner + step - place) for step in range(inner + 1)]
    ).astype(jnp.int32)
    total = multiply(blocks, options, block_of, choice_of, panel)
    end = count - 1
    multiples, sums_of = None, []
    for index in range(len(spans)):
        multiples, row_sums = multiply(
            [[block[index]] for block in [ups[end]] + downs[1:]],
            [tuple(range(count))],
            block_at(end).reshape(1).astype(jnp.int32),
            jnp.where(end <= place, 0, end - place).reshape(1).astype(jnp.int32),
            panel,
            spans[index][0],
            (total, data, multiples),
        )
        lines = (spans[index][1] - spans[index][0]) // LINE
        sums_of.append(row_sums.transpose(1, 0, 2, 3).reshape(3, lines, block_cols, LINE).sum(axis=3))

    sums = with_halo(jnp.concatenate(sums_of, axis=1), (("src", 1), ("rcv", 2)), 1)
    window = jnp.zeros((3, block_rows, block_cols), jnp.float32)
    for shift_row in range(3):
        for shift_col in range(3):
            window = (
                window
                + sums[:, shift_row : shift_row + block_rows, shift_col : shift_col + block_cols]
            )
    return match(multiples, jnp.repeat(window[:2] / (window[2:] + stabiliser), LINE, axis=2))


def solution(mesh):
    in_specs = (P(None, "src", "rcv"), P(None, "src"))
    out_specs = P(None, "src", "rcv")
    return jax.shard_map(
        on_device, mesh=mesh, in_specs=in_specs, out_specs=out_specs, check_vma=False
    )
```
